32 devices in a mesh: pole: 2 (over y), row: 4 (over z), col: 4 (over x, core).
Axes of the slice: x: 2, y: 2, z: 4, core: 2. Of those that a mesh axis runs over, the one named last changes fastest.
Arguments:
- inverse_top: bfloat16 [2048, 1024], P(('pole', 'row'), 'col'), parts along dimension 0
- factor_first: bfloat16 [8, 256, 1024], P(('pole', 'col'), 'row'), parts along dimension 0, may hold values from -0.75 to 0.75
- factor_second: bfloat16 [8, 256, 1024], P(('pole', 'col'), 'row'), parts along dimension 0, may hold values from -0.75 to 0.75
- parent_factor: bfloat16 [2048, 256], P(('pole', 'col')), parts along dimension 0, may hold values from -0.75 to 0.75
- diag_first_inv: float32 [2048, 256], P(('pole', 'col')), parts along dimension 0, may hold values from -6 to 6
- diag_second_inv: float32 [2048, 256], P(('pole', 'col')), parts along dimension 0, may hold values from -6 to 6
- pattern_first: int32 [4, 4], replicated, may hold values 0 or 1
- pattern_second: int32 [4, 4], replicated, may hold values 0 or 1
- parent: int32 [4, 1], replicated, may hold values from 0 to 3
Outputs:
- x_first: bfloat16 [2048, 1024], P(('pole', 'row'), 'col'), parts along dimension 0
- diag_first: bfloat16 [2048, 256], P(('pole', 'col')), parts along dimension 0
- x_second: bfloat16 [2048, 1024], P(('pole', 'row'), 'col'), parts along dimension 0
- cross_second: bfloat16 [2048, 256], P(('pole', 'col')), parts along dimension 0
- diag_second: float32 [2048, 256], P(('pole', 'col')), parts along dimension 0
The draws below stay inside these ranges and needn't reach their ends.
There are 2 independent parts, one for each index of `pole`. The reference program is written for one: setup_inputs(seed, part) draws one part's arguments, and reference() takes and returns one part's arrays. A program takes and returns all parts, laid end to end along the dimension named above; an argument that names none is the same for every part. Nothing has to cross between parts.
Inputs may be any that keep to these rules, and one draw needn't show every extreme that they name: `pattern_first`: 1 where the block row lies in the supernode's structure. `pattern_second`: 1 where the block row may lie in the supernode's structure. Every level-one supernode is the parent of some level-two supernode.
All inputs are finite; a program needn't handle non-finite values.
Results may differ from the reference program's by a relative error of at most 0.0053.
Values may be sent and summed in bfloat16 or wider, within the bound.
A program may use at most 64 MiB of HBM per device.

```python
import math
import jax
import jax.numpy as jnp
from jax import lax

W = 256
NB = 4
NS = 1024
M1 = 4
M2 = 4


def draw_inverse_top(key, part):
    first_key = jax.random.fold_in(key, 0)
    noise = jax.random.normal(first_key, (NS, NS), jnp.float32)
    matrix = (noise + noise.T) * (1.5 / math.sqrt(2.0 * NS)) + jnp.eye(NS, dtype=jnp.float32)
    return matrix.astype(jnp.bfloat16)


def touch_ends(result, stream_key, low, top_value):
    shape = result.shape
    place = [jax.random.randint(jax.random.fold_in(stream_key, axis), (), 0, shape[axis]) for axis in range(len(shape))]
    result = result.at[tuple(place)].set(low)
    longest = shape.index(max(shape))
    place[longest] = (place[longest] + 1) % shape[longest]
    return result.at[tuple(place)].set(top_value)


def block_levels(own_key, dims, cuts, least, top_value):
    def one(position, blocks):
        draws = jax.random.uniform(jax.random.fold_in(jax.random.fold_in(own_key, 6), position), (blocks,), jnp.float32, least / len(cuts), top_value / len(cuts))
        return jnp.repeat(jnp.exp(draws), dims[position] // blocks).reshape((-1,) + (1,) * (len(dims) - position - 1))

    factor_of = one(*cuts[0])
    for cut in cuts[1:]:
        factor_of = factor_of * one(*cut)
    return factor_of


def picks_of(rng, rows, amount, top, lift):
    order = jax.random.permutation(jax.random.fold_in(rng, 1), amount)
    boost = order
    for power in range(3):
        boost = boost * boost // amount
    boost = boost * lift // amount
    tickets = jax.random.randint(jax.random.fold_in(rng, 2), (rows, amount), 0, 4096) + boost
    holders = jax.random.permutation(jax.random.fold_in(rng, 3), rows)[jnp.arange(amount) % rows]
    tickets = jnp.where(jnp.arange(rows)[:, None] == holders[None, :], 1 << 14, tickets)
    score = tickets * amount + jnp.arange(amount)
    return lax.top_k(score.astype(jnp.int32), top)[1].astype(jnp.int32)


def bell_draw(own_key, shape, deviation, limit, shards=(), held_as=jnp.bfloat16):
    loudness = block_levels(own_key, shape, shards, -0.22, 0.18) if shards else 1.0
    drawn = jax.random.normal(own_key, shape, jnp.float32) * deviation * loudness
    return jnp.minimum(jnp.maximum(drawn, -limit), limit).astype(held_as)


def setup_inputs(seed: int = 0, part: int = 0) -> dict:
    seeds = jax.random.split(jax.random.key(seed), 10)
    part_splits = jax.random.split(jax.random.fold_in(seeds[9], part), 10)
    return {
        "inverse_top": draw_inverse_top(jax.random.fold_in(jax.random.fold_in(seeds[9], part), 71), part),
        "factor_first": bell_draw(part_splits[1], (NB, W, M1 * W), 0.125, 0.75, ((0, 4), (1, 4))),
        "factor_second": bell_draw(part_splits[2], (NB, W, M2 * W), 0.125, 0.75, ((0, 4), (1, 4))),
        "parent_factor": bell_draw(part_splits[3], (M2 * W, W), 0.125, 0.75, ((0, 4),)),
        "diag_first_inv": bell_draw(part_splits[4], (M1 * W, W), 1.0, 6.0, ((0, 4),), jnp.float32),
        "diag_second_inv": bell_draw(part_splits[5], (M2 * W, W), 1.0, 6.0, ((0, 4),), jnp.float32),
        "pattern_first": touch_ends((jax.random.randint(seeds[6], (NB, M1), 0, 2) < 1).astype(jnp.int32), jax.random.fold_in(seeds[6], 1), 0, 1),
        "pattern_second": touch_ends((jax.random.randint(seeds[7], (NB, M2), 0, 2) < 1).astype(jnp.int32), jax.random.fold_in(seeds[7], 1), 0, 1),
        "parent": picks_of(seeds[8], M2, M1, 1, 0),
    }


def spread_rows(pattern):
    return jnp.repeat(pattern, W, axis=1)


def reference(inverse_top, factor_first, factor_second, parent_factor, diag_first_inv, diag_second_inv, pattern_first, pattern_second, parent):
    onehot = (parent == jnp.arange(M1, dtype=jnp.int32)[None, :]).astype(jnp.int32)
    mask_second = pattern_second * jnp.sum(pattern_first[:, None, :] * onehot[None, :, :], axis=2)
    y_first = (factor_first * spread_rows(pattern_first).astype(jnp.bfloat16)[:, None, :]).reshape(NS, M1 * W)
    z_first = jnp.dot(inverse_top, y_first, preferred_element_type=jnp.float32)
    full_first = jnp.repeat(spread_rows(pattern_first), W, axis=0).astype(jnp.float32)
    x_first = (-(full_first * z_first)).astype(jnp.bfloat16)
    inner_first = jnp.einsum("nka,nkb->kab", y_first.reshape(NS, M1, W).astype(jnp.float32), x_first.reshape(NS, M1, W).astype(jnp.float32), precision=lax.Precision.HIGHEST)
    diag_first = (diag_first_inv.reshape(M1, W, W) - inner_first).astype(jnp.bfloat16)
    y_second = (factor_second * spread_rows(mask_second).astype(jnp.bfloat16)[:, None, :]).reshape(NS, M2 * W)
    parent_index = parent[:, 0]
    x_parent = x_first.reshape(NS, M1, W)[:, parent_index, :].astype(jnp.float32)
    below = parent_factor.reshape(M2, W, W).astype(jnp.float32)
    z_second = jnp.dot(inverse_top, y_second, preferred_element_type=jnp.float32)
    z_second = z_second + jnp.einsum("nja,jab->njb", x_parent, below, precision=lax.Precision.HIGHEST).reshape(NS, M2 * W)
    full_second = jnp.repeat(spread_rows(mask_second), W, axis=0).astype(jnp.float32)
    x_second = (-(full_second * z_second)).astype(jnp.bfloat16)
    y_blocks = y_second.reshape(NS, M2, W).astype(jnp.float32)
    cross_part = jnp.einsum("nja,njb->jab", x_parent, y_blocks, precision=lax.Precision.HIGHEST)
    a_parent = diag_first[parent_index].astype(jnp.float32)
    cross = (-(cross_part + jnp.einsum("jak,jkb->jab", a_parent, below, precision=lax.Precision.HIGHEST))).astype(jnp.bfloat16)
    inner_second = jnp.einsum("nja,njb->jab", y_blocks, x_second.reshape(NS, M2, W).astype(jnp.float32), precision=lax.Precision.HIGHEST)
    diag_second = diag_second_inv.reshape(M2, W, W) - inner_second - jnp.einsum("jab,jac->jbc", below, cross.astype(jnp.float32), precision=lax.Precision.HIGHEST)
    return (x_first, diag_first.reshape(M1 * W, W), x_second, cross.reshape(M2 * W, W), diag_second.reshape(M2 * W, W))
```

```python
import functools

import jax
import jax.numpy as jnp
from jax import lax
from jax.experimental import pallas as pl
from jax.experimental.pallas import tpu as pltpu
from jax.sharding import PartitionSpec as P


def broadcast(value, axis, source):
    kept = jnp.where(lax.axis_index(axis) == source, value, 0).astype(value.dtype)
    return lax.psum(kept, axis)


def spread_factor(masked):
    return lax.all_gather(masked, "row", axis=1, tiled=True)


def column_sums(parts):
    return lax.psum(parts, "row")


def on_device_large(
    inverse_top,
    factor_first,
    factor_second,
    parent_factor,
    diag_first_inv,
    diag_second_inv,
    pattern_first,
    pattern_second,
    parent,
):
    f32 = jnp.float32
    bf16 = jnp.bfloat16
    col_index = lax.axis_index("col")
    row_index = lax.axis_index("row")
    width = inverse_top.shape[0]
    blocks_col = factor_first.shape[0]
    local_first = diag_first_inv.shape[0] // width
    local_second = diag_second_inv.shape[0] // width
    total_first = pattern_first.shape[1]
    onehot = (parent == jnp.arange(total_first, dtype=jnp.int32)[None, :]).astype(jnp.int32)
    mask_second = pattern_second * jnp.sum(pattern_first[:, None, :] * onehot[None, :, :], axis=2)

    def column_mask(pattern):
        rows_here = lax.dynamic_slice_in_dim(pattern, col_index * blocks_col, blocks_col, 0)
        return jnp.repeat(rows_here, width, axis=1).astype(bf16)[:, None, :]

    def row_mask(pattern, count):
        piece = lax.dynamic_slice(pattern, (row_index, col_index * count), (1, count))
        return jnp.repeat(piece, width, axis=1).astype(f32)

    def owner_block(gathered, count):
        root = row_index // blocks_col
        pick = jnp.clip(row_index - col_index * blocks_col, 0, blocks_col - 1)
        own_all = broadcast(
            lax.dynamic_index_in_dim(gathered, pick, 0, keepdims=False), "col", root
        )
        return lax.dynamic_slice_in_dim(own_all, col_index * count * width, count * width, 1)

    def level_products(gathered, count):
        flat = gathered.reshape(-1, gathered.shape[2])
        summed = lax.psum_scatter(
            lax.dot_general(
                flat, inverse_top, (((0,), (1,)), ((), ())), preferred_element_type=f32
            ),
            "col",
            scatter_dimension=0,
            tiled=True,
        )
        own = owner_block(gathered, count)
        return (summed.T, own)

    masked_first = factor_first * column_mask(pattern_first)
    masked_second = factor_second * column_mask(mask_second)
    gathered_first = spread_factor(masked_first)
    z_first, own_first = level_products(gathered_first, local_first)
    x_first = (-(row_mask(pattern_first, local_first) * z_first)).astype(bf16)
    shape_first = (width, local_first, width)
    partial_first = jnp.einsum(
        "wsa,wsb->sab",
        own_first.reshape(shape_first),
        x_first.reshape(shape_first),
        preferred_element_type=f32,
    )
    summed_first = column_sums(partial_first)
    diag_first = (
        (diag_first_inv.reshape(local_first, width, width) - summed_first)
        .astype(bf16)
        .reshape(-1, width)
    )
    x_all, diag_all = (
        lax.all_gather(x_first, "col", axis=1, tiled=True),
        lax.all_gather(diag_first, "col", axis=0, tiled=True),
    )
    parent_here = lax.dynamic_slice_in_dim(parent, col_index * local_second, local_second, 0)
    select = (parent_here == jnp.arange(total_first, dtype=jnp.int32)[None, :]).astype(bf16)
    x_parent = jnp.einsum(
        "wkb,sk->wsb", x_all.reshape(width, total_first, width), select, preferred_element_type=f32
    ).astype(bf16)
    a_parent = jnp.einsum(
        "kab,sk->sab",
        diag_all.reshape(total_first, width, width),
        select,
        preferred_element_type=f32,
    ).astype(bf16)
    gathered_second = spread_factor(masked_second)
    z_second, own_second = level_products(gathered_second, local_second)
    below = parent_factor.reshape(local_second, width, width)
    z_second = z_second + jnp.einsum(
        "wsa,sab->wsb", x_parent, below, preferred_element_type=f32
    ).reshape(width, -1)
    x_second = (-(row_mask(mask_second, local_second) * z_second)).astype(bf16)
    shape_second = (width, local_second, width)
    own_blocks = own_second.reshape(shape_second)
    cross_part, inner_part = column_sums(
        (
            jnp.einsum("wsa,wsb->sab", x_parent, own_blocks, preferred_element_type=f32),
            jnp.einsum(
                "wsa,wsb->sab",
                own_blocks,
                x_second.reshape(shape_second),
                preferred_element_type=f32,
            ),
        )
    )
    cross = (
        -(cross_part + jnp.einsum("sak,skb->sab", a_parent, below, preferred_element_type=f32))
    ).astype(bf16)
    diag_second = (
        diag_second_inv.reshape(local_second, width, width)
        - inner_part
        - jnp.einsum("sab,sac->sbc", below, cross, preferred_element_type=f32)
    )
    return (x_first, diag_first, x_second, cross.reshape(-1, width), diag_second.reshape(-1, width))


MESH = pl.DeviceIdType.MESH
VMEM_BUDGET = 48 * 1024 * 1024
UP, DOWN, ACROSS, SIB, SIB_FAR = range(5)
INV, ONE, TWO, DIAG = range(4)


def fused_kernel(
    rows,
    cols,
    inv_ref,
    one_ref,
    two_ref,
    below_ref,
    dinv_one_ref,
    dinv_two_ref,
    pat_one,
    pat_two,
    parent,
    x_one_ref,
    diag_one_ref,
    x_two_ref,
    cross_ref,
    diag_two_ref,
    inv_all,
    one_all,
    two_all,
    diag_all,
    masked,
    x_one_all,
    x_two_all,
    send_sem,
    recv_sem,
    local_sem,
):
    f32, bf16 = jnp.float32, jnp.bfloat16
    width = inv_ref.shape[0]
    slab = one_ref.shape[0]
    y = lax.axis_index("pole")
    z = lax.axis_index("row")
    c = lax.axis_index("col")
    sib = c + 1 - 2 * (c % 2)
    far = (c + 2) % cols
    far_sib = (sib + 2) % cols
    devices = {
        UP: (y, z + 1, c),
        DOWN: (y, z - 1, c),
        ACROSS: (y, z, far),
        SIB: (y, z, sib),
        SIB_FAR: (y, z, sib),
    }

    def span(start, size):
        return pl.ds(pl.multiple_of(start, size), size)

    def columns(lane):
        if lane in (UP, DOWN):
            return slice(None)
        if lane == ACROSS:
            return span((far // 2) * 2 * width, 2 * width)
        return span(sib * width, width)

    def arrived(lane):
        if lane in (UP, DOWN):
            return slice(None)
        if lane == ACROSS:
            return span((c // 2) * 2 * width, 2 * width)
        return span(c * width, width)

    def place(unit, zs, cs, part):
        if unit == INV:
            return inv_all.at[cs, span(zs * width, width), :]
        if unit == ONE:
            return one_all.at[cs, zs]
        if unit == TWO:
            return two_all.at[cs, zs, :, part]
        return diag_all.at[cs]

    def origin(unit, part):
        if unit == INV:
            return inv_ref
        if unit == ONE:
            return one_ref
        if unit == TWO:
            return two_ref.at[:, part]
        return diag_all.at[c]

    def when(conditions, act):
        if conditions:
            both = conditions[0]
            for condition in conditions[1:]:
                both = jnp.logical_and(both, condition)
            pl.when(both)(act)
        else:
            act()

    sent = []

    def send(unit, zs, cs, lane, own=False, conditions=()):
        def descriptor():
            part = columns(lane)
            return pltpu.make_async_remote_copy(
                src_ref=origin(unit, part) if own else place(unit, zs, cs, part),
                dst_ref=place(unit, zs, cs, part),
                send_sem=send_sem.at[unit, zs, lane],
                recv_sem=recv_sem.at[unit, zs, cs],
                device_id=devices[lane],
                device_id_type=MESH,
            )

        when(list(conditions), lambda: descriptor().start())
        sent.append((list(conditions), descriptor))

    def receive(unit, zs, cs, lane, conditions=()):
        def act():
            part = arrived(lane)
            pltpu.make_async_remote_copy(
                src_ref=place(unit, zs, cs, part),
                dst_ref=place(unit, zs, cs, part),
                send_sem=send_sem.at[unit, zs, lane],
                recv_sem=recv_sem.at[unit, zs, cs],
                device_id=devices[SIB],
                device_id_type=MESH,
            ).wait_recv()

        when(list(conditions), act)

    can_up, can_down = z + 1 < rows, z >= 1
    diag_all[c] = dinv_one_ref[...].astype(bf16)

    barrier = pltpu.get_barrier_semaphore()
    for lane, conditions in ((UP, [can_up]), (DOWN, [can_down]), (ACROSS, []), (SIB, [])):
        when(
            conditions,
            lambda lane=lane: pl.semaphore_signal(
                barrier, inc=1, device_id=devices[lane], device_id_type=MESH
            ),
        )
    pl.semaphore_wait(barrier, 2 + can_up.astype(jnp.int32) + can_down.astype(jnp.int32))

    for unit in (INV, ONE, TWO):
        send(unit, z, c, UP, True, [can_up])
        send(unit, z, c, DOWN, True, [can_down])
        send(unit, z, c, ACROSS, True)
        send(unit, z, c, SIB, True)
    local = []
    for unit in (INV, ONE, TWO):
        local.append(
            pltpu.make_async_copy(
                origin(unit, slice(None)), place(unit, z, c, slice(None)), local_sem.at[unit]
            )
        )
        local[-1].start()
    send(DIAG, 0, c, ACROSS, True)
    send(DIAG, 0, c, SIB, True)

    def at_distance(step):
        if step == 0:
            return [(z, [], None, [])]
        return [
            (z - step, [z - step >= 0], UP, [can_up]),
            (z + step, [z + step < rows], DOWN, [can_down]),
        ]

    def pass_across(step):
        for unit in (INV, ONE, TWO):
            for zs, exists, _, _ in at_distance(step):
                receive(unit, zs, far, ACROSS, exists)
                send(unit, zs, far, SIB_FAR, False, exists)

    for step in range(1, rows):
        for unit in (INV, ONE, TWO):
            for zs, exists, lane, further in at_distance(step):
                receive(unit, zs, c, lane, exists)
                if step < rows - 1:
                    send(unit, zs, c, lane, False, exists + further)
                send(unit, zs, c, ACROSS, False, exists)
                send(unit, zs, c, SIB, False, exists)
        pass_across(step - 1)
        if step == 1:
            receive(DIAG, 0, far, ACROSS)
            send(DIAG, 0, far, SIB_FAR)
    pass_across(rows - 1)
    for unit in (INV, ONE, TWO):
        for zs in range(rows):
            receive(unit, zs, sib, SIB)
            receive(unit, zs, far_sib, SIB_FAR)
    receive(DIAG, 0, sib, SIB)
    receive(DIAG, 0, far_sib, SIB_FAR)
    for copy in local:
        copy.wait()

    chosen = [(parent[c, 0] == k).astype(jnp.int32).astype(f32) for k in range(cols)]

    def mask_one(b):
        return pat_one[b, c].astype(f32)

    def mask_parent(b):
        return sum(chosen[k] * pat_one[b, k].astype(f32) for k in range(cols))

    def mask_two(b):
        return pat_two[b, c].astype(f32) * mask_parent(b)

    def gather_columns(slot, source, mask):
        for b in range(cols):
            block = source[b, :, :, span(c * width, width)].reshape(width, width)
            masked[slot, b] = (block.astype(f32) * mask(b)).astype(bf16)

    def gather_parent():
        for b in range(cols):
            total = None
            for k in range(cols):
                block = one_all[b, :, :, k * width : (k + 1) * width].reshape(width, width)
                term = block.astype(f32) * (chosen[k] * pat_one[b, k].astype(f32))
                total = term if total is None else total + term
            masked[1, b] = total.astype(bf16)

    def dot(a, b, ca=1, cb=0):
        return lax.dot_general(a, b, (((ca,), (cb,)), ((), ())), preferred_element_type=f32)

    def times_inverse(slot, r):
        total = None
        for b in range(cols):
            term = dot(inv_all[b, r * width : (r + 1) * width, :], masked[slot, b])
            total = term if total is None else total + term
        return total

    gather_columns(0, one_all, mask_one)
    gather_parent()
    gather_columns(2, two_all, mask_two)
    below = below_ref[...]

    inner = jnp.zeros((width, width), f32)
    inner_parent = jnp.zeros((width, width), f32)
    for r in range(rows):
        x_own = (-(mask_one(r) * times_inverse(0, r))).astype(bf16)
        x_one_all[r] = x_own
        inner += dot(masked[0, r], x_own, 0, 0)
        x_par = (-(mask_parent(r) * times_inverse(1, r))).astype(bf16)
        x_two_all[r] = x_par
        inner_parent += dot(masked[1, r], x_par, 0, 0)
    x_one_ref[...] = x_one_all[z]
    diag_one_ref[...] = (dinv_one_ref[...] - inner).astype(bf16)
    dinv_parent = sum(chosen[k] * diag_all[k].astype(f32) for k in range(cols))
    diag_parent = (dinv_parent - inner_parent).astype(bf16)

    cross_part = dot(diag_parent, below)
    inner_two = jnp.zeros((width, width), f32)
    for r in range(rows):
        x_par = x_two_all[r]
        cross_part += dot(x_par, masked[2, r], 0, 0)
        z_two = times_inverse(2, r) + dot(x_par, below)
        x_two = (-(mask_two(r) * z_two)).astype(bf16)
        x_two_all[r] = x_two
        inner_two += dot(masked[2, r], x_two, 0, 0)
    x_two_ref[...] = x_two_all[z]
    cross = (-cross_part).astype(bf16)
    cross_ref[...] = cross
    diag_two_ref[...] = dinv_two_ref[...] - inner_two - dot(below, cross, 0, 0)

    for conditions, descriptor in sent:
        when(conditions, lambda descriptor=descriptor: descriptor().wait_send())


def on_device_small(
    rows,
    cols,
    inverse_top,
    factor_first,
    factor_second,
    parent_factor,
    diag_first_inv,
    diag_second_inv,
    pattern_first,
    pattern_second,
    parent,
):
    bf16 = jnp.bfloat16
    width = inverse_top.shape[0]
    slab, wide = factor_first.shape[1:]
    square = (width, width)
    vmem = pl.BlockSpec(memory_space=pltpu.VMEM)
    smem = pl.BlockSpec(memory_space=pltpu.SMEM)
    shape = jax.ShapeDtypeStruct
    return pl.pallas_call(
        functools.partial(fused_kernel, rows, cols),
        out_shape=(
            shape(square, bf16),
            shape(square, bf16),
            shape(square, bf16),
            shape(square, bf16),
            shape(square, jnp.float32),
        ),
        in_specs=[vmem] * 6 + [smem] * 3,
        out_specs=(vmem,) * 5,
        scratch_shapes=[
            pltpu.VMEM((cols, rows * width, width), bf16),
            pltpu.VMEM((cols, rows, slab, wide), bf16),
            pltpu.VMEM((cols, rows, slab, wide), bf16),
            pltpu.VMEM((cols,) + square, bf16),
            pltpu.VMEM((3, cols) + square, bf16),
            pltpu.VMEM((rows,) + square, bf16),
            pltpu.VMEM((rows,) + square, bf16),
            pltpu.SemaphoreType.DMA((4, rows, 5)),
            pltpu.SemaphoreType.DMA((4, rows, cols)),
            pltpu.SemaphoreType.DMA((3,)),
        ],
        compiler_params=pltpu.CompilerParams(
            collective_id=0, has_side_effects=True, vmem_limit_bytes=VMEM_BUDGET
        ),
    )(
        inverse_top,
        factor_first.reshape(slab, wide),
        factor_second.reshape(slab, wide),
        parent_factor,
        diag_first_inv,
        diag_second_inv,
        pattern_first,
        pattern_second,
        parent,
    )


def on_device(rows, cols, *args):
    inverse_top, factor_first, factor_second, parent_factor = args[:4]
    width, depth = inverse_top.shape
    one_each = (
        cols == 4
        and depth == width
        and factor_first.shape[0] == 1
        and factor_second.shape == factor_first.shape
        and factor_first.shape[1] % 16 == 0
        and factor_first.shape[2] == cols * width
        and parent_factor.shape[0] == width
        and rows == cols
    )
    gathered = 2 * rows * cols * (inverse_top.size + factor_first.size + factor_second.size)
    if one_each and gathered <= VMEM_BUDGET // 2:
        return on_device_small(rows, cols, *args)
    return on_device_large(*args)


def solution(mesh):
    in_specs = (
        P(("pole", "row"), "col"),
        P(("pole", "col"), "row", None),
        P(("pole", "col"), "row", None),
        P(("pole", "col"), None),
        P(("pole", "col"), None),
        P(("pole", "col"), None),
        P(),
        P(),
        P(),
    )
    out_specs = (
        P(("pole", "row"), "col"),
        P(("pole", "col"), None),
        P(("pole", "row"), "col"),
        P(("pole", "col"), None),
        P(("pole", "col"), None),
    )
    return jax.shard_map(
        functools.partial(on_device, mesh.shape["row"], mesh.shape["col"]), mesh=mesh, in_specs=in_specs, out_specs=out_specs, check_vma=False
    )
```

```python
import functools

import jax
import jax.numpy as jnp
from jax import lax
from jax.experimental import pallas as pl
from jax.experimental.pallas import tpu as pltpu
from jax.sharding import PartitionSpec as P


def broadcast(value, axis, source):
    kept = jnp.where(lax.axis_index(axis) == source, value, 0).astype(value.dtype)
    return lax.psum(kept, axis)


def spread_factor(masked):
    return lax.all_gather(masked, "row", axis=1, tiled=True)


def column_sums(parts):
    return lax.psum(parts, "row")


def on_device_large(
    inverse_top,
    factor_first,
    factor_second,
    parent_factor,
    diag_first_inv,
    diag_second_inv,
    pattern_first,
    pattern_second,
    parent,
):
    f32 = jnp.float32
    bf16 = jnp.bfloat16
    col_index = lax.axis_index("col")
    row_index = lax.axis_index("row")
    width = inverse_top.shape[0]
    blocks_col = factor_first.shape[0]
    local_first = diag_first_inv.shape[0] // width
    local_second = diag_second_inv.shape[0] // width
    total_first = pattern_first.shape[1]
    onehot = (parent == jnp.arange(total_first, dtype=jnp.int32)[None, :]).astype(jnp.int32)
    mask_second = pattern_second * jnp.sum(pattern_first[:, None, :] * onehot[None, :, :], axis=2)

    def column_mask(pattern):
        rows_here = lax.dynamic_slice_in_dim(pattern, col_index * blocks_col, blocks_col, 0)
        return jnp.repeat(rows_here, width, axis=1).astype(bf16)[:, None, :]

    def row_mask(pattern, count):
        piece = lax.dynamic_slice(pattern, (row_index, col_index * count), (1, count))
        return jnp.repeat(piece, width, axis=1).astype(f32)

    def owner_block(gathered, count):
        root = row_index // blocks_col
        pick = jnp.clip(row_index - col_index * blocks_col, 0, blocks_col - 1)
        own_all = broadcast(
            lax.dynamic_index_in_dim(gathered, pick, 0, keepdims=False), "col", root
        )
        return lax.dynamic_slice_in_dim(own_all, col_index * count * width, count * width, 1)

    def level_products(gathered, count):
        flat = gathered.reshape(-1, gathered.shape[2])
        summed = lax.psum_scatter(
            lax.dot_general(
                flat, inverse_top, (((0,), (1,)), ((), ())), preferred_element_type=f32
            ),
            "col",
            scatter_dimension=0,
            tiled=True,
        )
        own = owner_block(gathered, count)
        return (summed.T, own)

    masked_first = factor_first * column_mask(pattern_first)
    masked_second = factor_second * column_mask(mask_second)
    gathered_first = spread_factor(masked_first)
    z_first, own_first = level_products(gathered_first, local_first)
    x_first = (-(row_mask(pattern_first, local_first) * z_first)).astype(bf16)
    shape_first = (width, local_first, width)
    partial_first = jnp.einsum(
        "wsa,wsb->sab",
        own_first.reshape(shape_first),
        x_first.reshape(shape_first),
        preferred_element_type=f32,
    )
    summed_first = column_sums(partial_first)
    diag_first = (
        (diag_first_inv.reshape(local_first, width, width) - summed_first)
        .astype(bf16)
        .reshape(-1, width)
    )
    x_all, diag_all = (
        lax.all_gather(x_first, "col", axis=1, tiled=True),
        lax.all_gather(diag_first, "col", axis=0, tiled=True),
    )
    parent_here = lax.dynamic_slice_in_dim(parent, col_index * local_second, local_second, 0)
    select = (parent_here == jnp.arange(total_first, dtype=jnp.int32)[None, :]).astype(bf16)
    x_parent = jnp.einsum(
        "wkb,sk->wsb", x_all.reshape(width, total_first, width), select, preferred_element_type=f32
    ).astype(bf16)
    a_parent = jnp.einsum(
        "kab,sk->sab",
        diag_all.reshape(total_first, width, width),
        select,
        preferred_element_type=f32,
    ).astype(bf16)
    gathered_second = spread_factor(masked_second)
    z_second, own_second = level_products(gathered_second, local_second)
    below = parent_factor.reshape(local_second, width, width)
    z_second = z_second + jnp.einsum(
        "wsa,sab->wsb", x_parent, below, preferred_element_type=f32
    ).reshape(width, -1)
    x_second = (-(row_mask(mask_second, local_second) * z_second)).astype(bf16)
    shape_second = (width, local_second, width)
    own_blocks = own_second.reshape(shape_second)
    cross_part, inner_part = column_sums(
        (
            jnp.einsum("wsa,wsb->sab", x_parent, own_blocks, preferred_element_type=f32),
            jnp.einsum(
                "wsa,wsb->sab",
                own_blocks,
                x_second.reshape(shape_second),
                preferred_element_type=f32,
            ),
        )
    )
    cross = (
        -(cross_part + jnp.einsum("sak,skb->sab", a_parent, below, preferred_element_type=f32))
    ).astype(bf16)
    diag_second = (
        diag_second_inv.reshape(local_second, width, width)
        - inner_part
        - jnp.einsum("sab,sac->sbc", below, cross, preferred_element_type=f32)
    )
    return (x_first, diag_first, x_second, cross.reshape(-1, width), diag_second.reshape(-1, width))


MESH = pl.DeviceIdType.MESH
VMEM_BUDGET = 48 * 1024 * 1024
UP, DOWN, ACROSS, SIB, SIB_FAR = range(5)
INV, ONE, TWO, DIAG = range(4)


def fused_kernel(
    rows,
    cols,
    inv_ref,
    one_ref,
    two_ref,
    below_ref,
    dinv_one_ref,
    dinv_two_ref,
    pat_one,
    pat_two,
    parent,
    x_one_ref,
    diag_one_ref,
    x_two_ref,
    cross_ref,
    diag_two_ref,
    inv_all,
    one_all,
    two_all,
    below_own,
    dinv_one,
    dinv_two,
    diag_all,
    masked,
    x_one_all,
    x_two_all,
    send_sem,
    recv_sem,
    local_sem,
):
    f32, bf16 = jnp.float32, jnp.bfloat16
    width = inv_ref.shape[0]
    slab = one_ref.shape[0]
    y = lax.axis_index("pole")
    z = lax.axis_index("row")
    c = lax.axis_index("col")
    sib = c + 1 - 2 * (c % 2)
    far = (c + 2) % cols
    far_sib = (sib + 2) % cols
    devices = {
        UP: (y, z + 1, c),
        DOWN: (y, z - 1, c),
        ACROSS: (y, z, far),
        SIB: (y, z, sib),
        SIB_FAR: (y, z, sib),
    }

    def span(start, size):
        return pl.ds(pl.multiple_of(start, size), size)

    def columns(lane):
        if lane in (UP, DOWN):
            return slice(None)
        if lane == ACROSS:
            return span((far // 2) * 2 * width, 2 * width)
        return span(sib * width, width)

    def arrived(lane):
        if lane in (UP, DOWN):
            return slice(None)
        if lane == ACROSS:
            return span((c // 2) * 2 * width, 2 * width)
        return span(c * width, width)

    def place(unit, zs, cs, part):
        if unit == INV:
            return inv_all.at[cs, span(zs * width, width), :]
        if unit == ONE:
            return one_all.at[cs, zs]
        if unit == TWO:
            return two_all.at[cs, zs, :, part]
        return diag_all.at[cs]

    def when(conditions, act):
        if conditions:
            both = conditions[0]
            for condition in conditions[1:]:
                both = jnp.logical_and(both, condition)
            pl.when(both)(act)
        else:
            act()

    sent = []

    def send(unit, zs, cs, lane, conditions=()):
        def descriptor():
            part = columns(lane)
            return pltpu.make_async_remote_copy(
                src_ref=place(unit, zs, cs, part),
                dst_ref=place(unit, zs, cs, part),
                send_sem=send_sem.at[unit, zs, lane],
                recv_sem=recv_sem.at[unit, zs, cs],
                device_id=devices[lane],
                device_id_type=MESH,
            )

        when(list(conditions), lambda: descriptor().start())
        sent.append((list(conditions), descriptor))

    def receive(unit, zs, cs, lane, conditions=()):
        def act():
            part = arrived(lane)
            pltpu.make_async_remote_copy(
                src_ref=place(unit, zs, cs, part),
                dst_ref=place(unit, zs, cs, part),
                send_sem=send_sem.at[unit, zs, lane],
                recv_sem=recv_sem.at[unit, zs, cs],
                device_id=devices[SIB],
                device_id_type=MESH,
            ).wait_recv()

        when(list(conditions), act)

    can_up, can_down = z + 1 < rows, z >= 1
    everything = slice(None)
    local = [
        pltpu.make_async_copy(source, target, local_sem.at[slot])
        for slot, (source, target) in enumerate(
            (
                (inv_ref, place(INV, z, c, everything)),
                (one_ref, place(ONE, z, c, everything)),
                (two_ref, place(TWO, z, c, everything)),
                (below_ref, below_own),
                (dinv_one_ref, dinv_one),
                (dinv_two_ref, dinv_two),
            )
        )
    ]
    for copy in local:
        copy.start()

    barrier = pltpu.get_barrier_semaphore()
    for lane, conditions in ((UP, [can_up]), (DOWN, [can_down]), (ACROSS, []), (SIB, [])):
        when(
            conditions,
            lambda lane=lane: pl.semaphore_signal(
                barrier, inc=1, device_id=devices[lane], device_id_type=MESH
            ),
        )
    pl.semaphore_wait(barrier, 2 + can_up.astype(jnp.int32) + can_down.astype(jnp.int32))

    def at_distance(step):
        if step == 0:
            return [(z, [], None, [])]
        return [
            (z - step, [z - step >= 0], UP, [can_up]),
            (z + step, [z + step < rows], DOWN, [can_down]),
        ]

    def send_own(unit):
        local[unit].wait()
        send(unit, z, c, UP, [can_up])
        send(unit, z, c, DOWN, [can_down])
        send(unit, z, c, ACROSS)
        send(unit, z, c, SIB)

    def pass_along(units, step):
        for unit in units:
            for zs, exists, lane, further in at_distance(step):
                receive(unit, zs, c, lane, exists)
                if step < rows - 1:
                    send(unit, zs, c, lane, exists + further)
                send(unit, zs, c, ACROSS, exists)
                send(unit, zs, c, SIB, exists)

    def pass_across(units, step):
        for unit in units:
            for zs, exists, _, _ in at_distance(step):
                receive(unit, zs, far, ACROSS, exists)
                send(unit, zs, far, SIB_FAR, exists)

    def settle(units):
        for unit in units:
            for zs in range(rows):
                receive(unit, zs, sib, SIB)
                receive(unit, zs, far_sib, SIB_FAR)

    first = (INV, ONE)
    for unit in first:
        send_own(unit)
    for step in range(1, rows):
        if step == rows - 1:
            send_own(TWO)
        pass_along(first, step)
        pass_across(first, step - 1)
    for step in range(1, rows - 1):
        pass_along((TWO,), step)
    pass_across(first, rows - 1)
    settle(first)
    for copy in local[3:]:
        copy.wait()

    chosen = [(parent[c, 0] == k).astype(jnp.int32).astype(f32) for k in range(cols)]

    def mask_one(b):
        return pat_one[b, c].astype(f32)

    def mask_parent(b):
        return sum(chosen[k] * pat_one[b, k].astype(f32) for k in range(cols))

    def mask_two(b):
        return pat_two[b, c].astype(f32) * mask_parent(b)

    def gather_columns(slot, source, mask):
        for b in range(cols):
            block = source[b, :, :, span(c * width, width)].reshape(width, width)
            masked[slot, b] = (block.astype(f32) * mask(b)).astype(bf16)

    def gather_parent():
        for b in range(cols):
            total = None
            for k in range(cols):
                block = one_all[b, :, :, k * width : (k + 1) * width].reshape(width, width)
                term = block.astype(f32) * (chosen[k] * pat_one[b, k].astype(f32))
                total = term if total is None else total + term
            masked[1, b] = total.astype(bf16)

    def dot(a, b, ca=1, cb=0):
        return lax.dot_general(a, b, (((ca,), (cb,)), ((), ())), preferred_element_type=f32)

    def times_inverse(slot, r):
        total = None
        for b in range(cols):
            term = dot(inv_all[b, r * width : (r + 1) * width, :], masked[slot, b])
            total = term if total is None else total + term
        return total

    gather_columns(0, one_all, mask_one)
    gather_parent()
    below = below_own[...]

    inner = jnp.zeros((width, width), f32)
    for r in range(rows):
        x_own = (-(mask_one(r) * times_inverse(0, r))).astype(bf16)
        x_one_all[r] = x_own
        inner += dot(masked[0, r], x_own, 0, 0)
    diag_one = (dinv_one[...] - inner).astype(bf16)
    diag_all[c] = diag_one
    send(DIAG, 0, c, ACROSS)
    send(DIAG, 0, c, SIB)
    pass_along((TWO,), rows - 1)
    for r in range(rows):
        x_two_all[r] = (-(mask_parent(r) * times_inverse(1, r))).astype(bf16)
    for step in range(rows):
        pass_across((TWO,), step)
    receive(DIAG, 0, far, ACROSS)
    send(DIAG, 0, far, SIB_FAR)
    x_one_ref[...] = x_one_all[z]
    diag_one_ref[...] = diag_one
    settle((TWO,))
    gather_columns(2, two_all, mask_two)

    cross_part = jnp.zeros((width, width), f32)
    inner_two = jnp.zeros((width, width), f32)
    for r in range(rows):
        x_par = x_two_all[r]
        cross_part += dot(x_par, masked[2, r], 0, 0)
        z_two = times_inverse(2, r) + dot(x_par, below)
        x_two = (-(mask_two(r) * z_two)).astype(bf16)
        x_two_all[r] = x_two
        inner_two += dot(masked[2, r], x_two, 0, 0)
    x_two_ref[...] = x_two_all[z]
    receive(DIAG, 0, sib, SIB)
    receive(DIAG, 0, far_sib, SIB_FAR)
    diag_parent = sum(chosen[k] * diag_all[k].astype(f32) for k in range(cols)).astype(bf16)
    cross = (-(cross_part + dot(diag_parent, below))).astype(bf16)
    cross_ref[...] = cross
    diag_two_ref[...] = dinv_two[...] - inner_two - dot(below, cross, 0, 0)

    for conditions, descriptor in sent:
        when(conditions, lambda descriptor=descriptor: descriptor().wait_send())


def on_device_small(
    rows,
    cols,
    inverse_top,
    factor_first,
    factor_second,
    parent_factor,
    diag_first_inv,
    diag_second_inv,
    pattern_first,
    pattern_second,
    parent,
):
    bf16 = jnp.bfloat16
    width = inverse_top.shape[0]
    slab, wide = factor_first.shape[1:]
    square = (width, width)
    vmem = pl.BlockSpec(memory_space=pltpu.VMEM)
    hbm = pl.BlockSpec(memory_space=pltpu.HBM)
    smem = pl.BlockSpec(memory_space=pltpu.SMEM)
    shape = jax.ShapeDtypeStruct
    return pl.pallas_call(
        functools.partial(fused_kernel, rows, cols),
        out_shape=(
            shape(square, bf16),
            shape(square, bf16),
            shape(square, bf16),
            shape(square, bf16),
            shape(square, jnp.float32),
        ),
        in_specs=[hbm] * 6 + [smem] * 3,
        out_specs=(vmem,) * 5,
        scratch_shapes=[
            pltpu.VMEM((cols, rows * width, width), bf16),
            pltpu.VMEM((cols, rows, slab, wide), bf16),
            pltpu.VMEM((cols, rows, slab, wide), bf16),
            pltpu.VMEM(square, bf16),
            pltpu.VMEM(square, jnp.float32),
            pltpu.VMEM(square, jnp.float32),
            pltpu.VMEM((cols,) + square, bf16),
            pltpu.VMEM((3, cols) + square, bf16),
            pltpu.VMEM((rows,) + square, bf16),
            pltpu.VMEM((rows,) + square, bf16),
            pltpu.SemaphoreType.DMA((4, rows, 5)),
            pltpu.SemaphoreType.DMA((4, rows, cols)),
            pltpu.SemaphoreType.DMA((6,)),
        ],
        compiler_params=pltpu.CompilerParams(
            collective_id=0, has_side_effects=True, vmem_limit_bytes=VMEM_BUDGET
        ),
    )(
        inverse_top,
        factor_first.reshape(slab, wide),
        factor_second.reshape(slab, wide),
        parent_factor,
        diag_first_inv,
        diag_second_inv,
        pattern_first,
        pattern_second,
        parent,
    )


def on_device(rows, cols, *args):
    inverse_top, factor_first, factor_second, parent_factor = args[:4]
    width, depth = inverse_top.shape
    one_each = (
        cols == 4
        and depth == width
        and factor_first.shape[0] == 1
        and factor_second.shape == factor_first.shape
        and factor_first.shape[1] % 16 == 0
        and factor_first.shape[2] == cols * width
        and parent_factor.shape[0] == width
        and rows == cols
    )
    gathered = 2 * rows * cols * (inverse_top.size + factor_first.size + factor_second.size)
    if one_each and gathered <= VMEM_BUDGET // 2:
        return on_device_small(rows, cols, *args)
    return on_device_large(*args)


def solution(mesh):
    in_specs = (
        P(("pole", "row"), "col"),
        P(("pole", "col"), "row", None),
        P(("pole", "col"), "row", None),
        P(("pole", "col"), None),
        P(("pole", "col"), None),
        P(("pole", "col"), None),
        P(),
        P(),
        P(),
    )
    out_specs = (
        P(("pole", "row"), "col"),
        P(("pole", "col"), None),
        P(("pole", "row"), "col"),
        P(("pole", "col"), None),
        P(("pole", "col"), None),
    )
    return jax.shard_map(
        functools.partial(on_device, mesh.shape["row"], mesh.shape["col"]), mesh=mesh, in_specs=in_specs, out_specs=out_specs, check_vma=False
    )
```

```python
import functools

import jax
import jax.numpy as jnp
from jax import lax
from jax.experimental import pallas as pl
from jax.experimental.pallas import tpu as pltpu
from jax.sharding import PartitionSpec as P


def broadcast(value, axis, source):
    kept = jnp.where(lax.axis_index(axis) == source, value, 0).astype(value.dtype)
    return lax.psum(kept, axis)


def spread_factor(masked):
    return lax.all_gather(masked, "row", axis=1, tiled=True)


def column_sums(parts):
    return lax.psum(parts, "row")


def on_device_large(
    inverse_top,
    factor_first,
    factor_second,
    parent_factor,
    diag_first_inv,
    diag_second_inv,
    pattern_first,
    pattern_second,
    parent,
):
    f32 = jnp.float32
    bf16 = jnp.bfloat16
    col_index = lax.axis_index("col")
    row_index = lax.axis_index("row")
    width = inverse_top.shape[0]
    blocks_col = factor_first.shape[0]
    local_first = diag_first_inv.shape[0] // width
    local_second = diag_second_inv.shape[0] // width
    total_first = pattern_first.shape[1]
    onehot = (parent == jnp.arange(total_first, dtype=jnp.int32)[None, :]).astype(jnp.int32)
    mask_second = pattern_second * jnp.sum(pattern_first[:, None, :] * onehot[None, :, :], axis=2)

    def column_mask(pattern):
        rows_here = lax.dynamic_slice_in_dim(pattern, col_index * blocks_col, blocks_col, 0)
        return jnp.repeat(rows_here, width, axis=1).astype(bf16)[:, None, :]

    def row_mask(pattern, count):
        piece = lax.dynamic_slice(pattern, (row_index, col_index * count), (1, count))
        return jnp.repeat(piece, width, axis=1).astype(f32)

    def owner_block(gathered, count):
        root = row_index // blocks_col
        pick = jnp.clip(row_index - col_index * blocks_col, 0, blocks_col - 1)
        own_all = broadcast(
            lax.dynamic_index_in_dim(gathered, pick, 0, keepdims=False), "col", root
        )
        return lax.dynamic_slice_in_dim(own_all, col_index * count * width, count * width, 1)

    def level_products(gathered, count):
        flat = gathered.reshape(-1, gathered.shape[2])
        summed = lax.psum_scatter(
            lax.dot_general(
                flat, inverse_top, (((0,), (1,)), ((), ())), preferred_element_type=f32
            ),
            "col",
            scatter_dimension=0,
            tiled=True,
        )
        own = owner_block(gathered, count)
        return (summed.T, own)

    masked_first = factor_first * column_mask(pattern_first)
    masked_second = factor_second * column_mask(mask_second)
    gathered_first = spread_factor(masked_first)
    z_first, own_first = level_products(gathered_first, local_first)
    x_first = (-(row_mask(pattern_first, local_first) * z_first)).astype(bf16)
    shape_first = (width, local_first, width)
    partial_first = jnp.einsum(
        "wsa,wsb->sab",
        own_first.reshape(shape_first),
        x_first.reshape(shape_first),
        preferred_element_type=f32,
    )
    summed_first = column_sums(partial_first)
    diag_first = (
        (diag_first_inv.reshape(local_first, width, width) - summed_first)
        .astype(bf16)
        .reshape(-1, width)
    )
    x_all, diag_all = (
        lax.all_gather(x_first, "col", axis=1, tiled=True),
        lax.all_gather(diag_first, "col", axis=0, tiled=True),
    )
    parent_here = lax.dynamic_slice_in_dim(parent, col_index * local_second, local_second, 0)
    select = (parent_here == jnp.arange(total_first, dtype=jnp.int32)[None, :]).astype(bf16)
    x_parent = jnp.einsum(
        "wkb,sk->wsb", x_all.reshape(width, total_first, width), select, preferred_element_type=f32
    ).astype(bf16)
    a_parent = jnp.einsum(
        "kab,sk->sab",
        diag_all.reshape(total_first, width, width),
        select,
        preferred_element_type=f32,
    ).astype(bf16)
    gathered_second = spread_factor(masked_second)
    z_second, own_second = level_products(gathered_second, local_second)
    below = parent_factor.reshape(local_second, width, width)
    z_second = z_second + jnp.einsum(
        "wsa,sab->wsb", x_parent, below, preferred_element_type=f32
    ).reshape(width, -1)
    x_second = (-(row_mask(mask_second, local_second) * z_second)).astype(bf16)
    shape_second = (width, local_second, width)
    own_blocks = own_second.reshape(shape_second)
    cross_part, inner_part = column_sums(
        (
            jnp.einsum("wsa,wsb->sab", x_parent, own_blocks, preferred_element_type=f32),
            jnp.einsum(
                "wsa,wsb->sab",
                own_blocks,
                x_second.reshape(shape_second),
                preferred_element_type=f32,
            ),
        )
    )
    cross = (
        -(cross_part + jnp.einsum("sak,skb->sab", a_parent, below, preferred_element_type=f32))
    ).astype(bf16)
    diag_second = (
        diag_second_inv.reshape(local_second, width, width)
        - inner_part
        - jnp.einsum("sab,sac->sbc", below, cross, preferred_element_type=f32)
    )
    return (x_first, diag_first, x_second, cross.reshape(-1, width), diag_second.reshape(-1, width))


MESH = pl.DeviceIdType.MESH
VMEM_BUDGET = 64 * 1024 * 1024
UP, DOWN, ACROSS, SIB, SIB_FAR = range(5)
INV, ONE, TWO, DIAG = range(4)


def fused_kernel(
    rows,
    cols,
    inv_ref,
    one_ref,
    two_ref,
    below_ref,
    dinv_one_ref,
    dinv_two_ref,
    pat_one,
    pat_two,
    parent,
    x_one_ref,
    diag_one_ref,
    x_two_ref,
    cross_ref,
    diag_two_ref,
    inv_all,
    one_all,
    two_all,
    below_own,
    dinv_one,
    dinv_two,
    diag_all,
    masked,
    x_one_all,
    x_two_all,
    send_sem,
    recv_sem,
    local_sem,
):
    f32, bf16 = jnp.float32, jnp.bfloat16
    width = inv_ref.shape[0]
    slab = one_ref.shape[0]
    y = lax.axis_index("pole")
    z = lax.axis_index("row")
    c = lax.axis_index("col")
    sib = c + 1 - 2 * (c % 2)
    far = (c + 2) % cols
    far_sib = (sib + 2) % cols
    devices = {
        UP: (y, z + 1, c),
        DOWN: (y, z - 1, c),
        ACROSS: (y, z, far),
        SIB: (y, z, sib),
        SIB_FAR: (y, z, sib),
    }

    def span(start, size):
        return pl.ds(pl.multiple_of(start, size), size)

    def columns(lane):
        if lane in (UP, DOWN):
            return slice(None)
        if lane == ACROSS:
            return span((far // 2) * 2 * width, 2 * width)
        return span(sib * width, width)

    def arrived(lane):
        if lane in (UP, DOWN):
            return slice(None)
        if lane == ACROSS:
            return span((c // 2) * 2 * width, 2 * width)
        return span(c * width, width)

    def place(unit, zs, cs, part):
        if unit == INV:
            return inv_all.at[cs, span(zs * width, width), :]
        if unit == ONE:
            return one_all.at[cs, zs]
        if unit == TWO:
            return two_all.at[cs, zs, :, part]
        return diag_all.at[cs]

    def when(conditions, act):
        if conditions:
            both = conditions[0]
            for condition in conditions[1:]:
                both = jnp.logical_and(both, condition)
            pl.when(both)(act)
        else:
            act()

    sent = []

    def send(unit, zs, cs, lane, conditions=()):
        def descriptor():
            part = columns(lane)
            return pltpu.make_async_remote_copy(
                src_ref=place(unit, zs, cs, part),
                dst_ref=place(unit, zs, cs, part),
                send_sem=send_sem.at[unit, zs, lane],
                recv_sem=recv_sem.at[unit, zs, cs],
                device_id=devices[lane],
                device_id_type=MESH,
            )

        when(list(conditions), lambda: descriptor().start())
        sent.append((list(conditions), descriptor))

    def receive(unit, zs, cs, lane, conditions=()):
        def act():
            part = arrived(lane)
            pltpu.make_async_remote_copy(
                src_ref=place(unit, zs, cs, part),
                dst_ref=place(unit, zs, cs, part),
                send_sem=send_sem.at[unit, zs, lane],
                recv_sem=recv_sem.at[unit, zs, cs],
                device_id=devices[SIB],
                device_id_type=MESH,
            ).wait_recv()

        when(list(conditions), act)

    can_up, can_down = z + 1 < rows, z >= 1
    everything = slice(None)
    local = [
        pltpu.make_async_copy(source, target, local_sem.at[slot])
        for slot, (source, target) in enumerate(
            (
                (inv_ref, place(INV, z, c, everything)),
                (one_ref, place(ONE, z, c, everything)),
                (two_ref, place(TWO, z, c, everything)),
                (below_ref, below_own),
                (dinv_one_ref, dinv_one),
                (dinv_two_ref, dinv_two),
            )
        )
    ]
    for copy in local:
        copy.start()

    barrier = pltpu.get_barrier_semaphore()
    for lane, conditions in ((UP, [can_up]), (DOWN, [can_down]), (ACROSS, []), (SIB, [])):
        when(
            conditions,
            lambda lane=lane: pl.semaphore_signal(
                barrier, inc=1, device_id=devices[lane], device_id_type=MESH
            ),
        )
    pl.semaphore_wait(barrier, 2 + can_up.astype(jnp.int32) + can_down.astype(jnp.int32))

    def at_distance(step):
        if step == 0:
            return [(z, [], None, [])]
        return [
            (z - step, [z - step >= 0], UP, [can_up]),
            (z + step, [z + step < rows], DOWN, [can_down]),
        ]

    def send_own(unit):
        local[unit].wait()
        send(unit, z, c, UP, [can_up])
        send(unit, z, c, DOWN, [can_down])
        send(unit, z, c, ACROSS)
        send(unit, z, c, SIB)

    def pass_along(units, step):
        for unit in units:
            for zs, exists, lane, further in at_distance(step):
                receive(unit, zs, c, lane, exists)
                if step < rows - 1:
                    send(unit, zs, c, lane, exists + further)
                send(unit, zs, c, ACROSS, exists)
                send(unit, zs, c, SIB, exists)

    def pass_across(units, step):
        for unit in units:
            for zs, exists, _, _ in at_distance(step):
                receive(unit, zs, far, ACROSS, exists)
                send(unit, zs, far, SIB_FAR, exists)

    def settle(units):
        for unit in units:
            for zs in range(rows):
                receive(unit, zs, sib, SIB)
                receive(unit, zs, far_sib, SIB_FAR)

    first = (INV, ONE)
    for unit in first:
        send_own(unit)
    for step in range(1, rows):
        if step == rows - 1:
            send_own(TWO)
        pass_along(first, step)
    for step in range(1, rows - 1):
        pass_along((TWO,), step)
    for step in range(rows):
        pass_across(first, step)
    settle(first)
    for copy in local[3:]:
        copy.wait()

    chosen = [(parent[c, 0] == k).astype(jnp.int32).astype(f32) for k in range(cols)]

    def mask_one(b):
        return pat_one[b, c].astype(f32)

    def mask_parent(b):
        return sum(chosen[k] * pat_one[b, k].astype(f32) for k in range(cols))

    def mask_two(b):
        return pat_two[b, c].astype(f32) * mask_parent(b)

    def gather_columns(slot, source, mask):
        for b in range(cols):
            block = source[b, :, :, span(c * width, width)].reshape(width, width)
            masked[slot, b] = (block.astype(f32) * mask(b)).astype(bf16)

    def gather_parent():
        for b in range(cols):
            total = None
            for k in range(cols):
                block = one_all[b, :, :, k * width : (k + 1) * width].reshape(width, width)
                term = block.astype(f32) * (chosen[k] * pat_one[b, k].astype(f32))
                total = term if total is None else total + term
            masked[1, b] = total.astype(bf16)

    def dot(a, b, ca=1, cb=0):
        return lax.dot_general(a, b, (((ca,), (cb,)), ((), ())), preferred_element_type=f32)

    def times_inverse(slot, r):
        total = None
        for b in range(cols):
            term = dot(inv_all[b, r * width : (r + 1) * width, :], masked[slot, b])
            total = term if total is None else total + term
        return total

    gather_columns(0, one_all, mask_one)
    gather_parent()
    below = below_own[...]

    inner = jnp.zeros((width, width), f32)
    for r in range(rows):
        x_own = (-(mask_one(r) * times_inverse(0, r))).astype(bf16)
        x_one_all[r] = x_own
        inner += dot(masked[0, r], x_own, 0, 0)
    diag_one = (dinv_one[...] - inner).astype(bf16)
    diag_all[c] = diag_one
    send(DIAG, 0, c, ACROSS)
    send(DIAG, 0, c, SIB)
    pass_along((TWO,), rows - 1)
    for r in range(rows):
        x_two_all[r] = (-(mask_parent(r) * times_inverse(1, r))).astype(bf16)
    for step in range(rows):
        pass_across((TWO,), step)
    receive(DIAG, 0, far, ACROSS)
    send(DIAG, 0, far, SIB_FAR)
    x_one_ref[...] = x_one_all[z]
    diag_one_ref[...] = diag_one
    settle((TWO,))
    gather_columns(2, two_all, mask_two)

    cross_part = jnp.zeros((width, width), f32)
    inner_two = jnp.zeros((width, width), f32)
    for r in range(rows):
        x_par = x_two_all[r]
        cross_part += dot(x_par, masked[2, r], 0, 0)
        z_two = times_inverse(2, r) + dot(x_par, below)
        x_two = (-(mask_two(r) * z_two)).astype(bf16)
        x_two_all[r] = x_two
        inner_two += dot(masked[2, r], x_two, 0, 0)
    x_two_ref[...] = x_two_all[z]
    receive(DIAG, 0, sib, SIB)
    receive(DIAG, 0, far_sib, SIB_FAR)
    diag_parent = sum(chosen[k] * diag_all[k].astype(f32) for k in range(cols)).astype(bf16)
    cross = (-(cross_part + dot(diag_parent, below))).astype(bf16)
    cross_ref[...] = cross
    diag_two_ref[...] = dinv_two[...] - inner_two - dot(below, cross, 0, 0)

    for conditions, descriptor in sent:
        when(conditions, lambda descriptor=descriptor: descriptor().wait_send())


def on_device_small(
    rows,
    cols,
    inverse_top,
    factor_first,
    factor_second,
    parent_factor,
    diag_first_inv,
    diag_second_inv,
    pattern_first,
    pattern_second,
    parent,
):
    bf16 = jnp.bfloat16
    width = inverse_top.shape[0]
    slab, wide = factor_first.shape[1:]
    square = (width, width)
    vmem = pl.BlockSpec(memory_space=pltpu.VMEM)
    hbm = pl.BlockSpec(memory_space=pltpu.HBM)
    smem = pl.BlockSpec(memory_space=pltpu.SMEM)
    shape = jax.ShapeDtypeStruct
    return pl.pallas_call(
        functools.partial(fused_kernel, rows, cols),
        out_shape=(
            shape(square, bf16),
            shape(square, bf16),
            shape(square, bf16),
            shape(square, bf16),
            shape(square, jnp.float32),
        ),
        in_specs=[hbm] * 6 + [smem] * 3,
        out_specs=(vmem,) * 5,
        scratch_shapes=[
            pltpu.VMEM((cols, rows * width, width), bf16),
            pltpu.VMEM((cols, rows, slab, wide), bf16),
            pltpu.VMEM((cols, rows, slab, wide), bf16),
            pltpu.VMEM(square, bf16),
            pltpu.VMEM(square, jnp.float32),
            pltpu.VMEM(square, jnp.float32),
            pltpu.VMEM((cols,) + square, bf16),
            pltpu.VMEM((3, cols) + square, bf16),
            pltpu.VMEM((rows,) + square, bf16),
            pltpu.VMEM((rows,) + square, bf16),
            pltpu.SemaphoreType.DMA((4, rows, 5)),
            pltpu.SemaphoreType.DMA((4, rows, cols)),
            pltpu.SemaphoreType.DMA((6,)),
        ],
        compiler_params=pltpu.CompilerParams(
            collective_id=0, has_side_effects=True, vmem_limit_bytes=VMEM_BUDGET
        ),
    )(
        inverse_top,
        factor_first.reshape(slab, wide),
        factor_second.reshape(slab, wide),
        parent_factor,
        diag_first_inv,
        diag_second_inv,
        pattern_first,
        pattern_second,
        parent,
    )


def on_device(rows, cols, *args):
    inverse_top, factor_first, factor_second, parent_factor = args[:4]
    width, depth = inverse_top.shape
    one_each = (
        cols == 4
        and depth == width
        and factor_first.shape[0] == 1
        and factor_second.shape == factor_first.shape
        and factor_first.shape[1] % 16 == 0
        and factor_first.shape[2] == cols * width
        and parent_factor.shape[0] == width
        and rows == cols
    )
    gathered = 2 * rows * cols * (inverse_top.size + factor_first.size + factor_second.size)
    if one_each and gathered <= VMEM_BUDGET // 2:
        return on_device_small(rows, cols, *args)
    return on_device_large(*args)


def solution(mesh):
    in_specs = (
        P(("pole", "row"), "col"),
        P(("pole", "col"), "row", None),
        P(("pole", "col"), "row", None),
        P(("pole", "col"), None),
        P(("pole", "col"), None),
        P(("pole", "col"), None),
        P(),
        P(),
        P(),
    )
    out_specs = (
        P(("pole", "row"), "col"),
        P(("pole", "col"), None),
        P(("pole", "row"), "col"),
        P(("pole", "col"), None),
        P(("pole", "col"), None),
    )
    return jax.shard_map(
        functools.partial(on_device, mesh.shape["row"], mesh.shape["col"]), mesh=mesh, in_specs=in_specs, out_specs=out_specs, check_vma=False
    )
```

```python
import functools

import jax
import jax.numpy as jnp
from jax import lax
from jax.experimental import pallas as pl
from jax.experimental.pallas import tpu as pltpu
from jax.sharding import PartitionSpec as P


def broadcast(value, axis, source):
    kept = jnp.where(lax.axis_index(axis) == source, value, 0).astype(value.dtype)
    return lax.psum(kept, axis)


def spread_factor(masked):
    return lax.all_gather(masked, "row", axis=1, tiled=True)


def column_sums(parts):
    return lax.psum(parts, "row")


def on_device_large(
    inverse_top,
    factor_first,
    factor_second,
    parent_factor,
    diag_first_inv,
    diag_second_inv,
    pattern_first,
    pattern_second,
    parent,
):
    f32 = jnp.float32
    bf16 = jnp.bfloat16
    col_index = lax.axis_index("col")
    row_index = lax.axis_index("row")
    width = inverse_top.shape[0]
    blocks_col = factor_first.shape[0]
    local_first = diag_first_inv.shape[0] // width
    local_second = diag_second_inv.shape[0] // width
    total_first = pattern_first.shape[1]
    onehot = (parent == jnp.arange(total_first, dtype=jnp.int32)[None, :]).astype(jnp.int32)
    mask_second = pattern_second * jnp.sum(pattern_first[:, None, :] * onehot[None, :, :], axis=2)

    def column_mask(pattern):
        rows_here = lax.dynamic_slice_in_dim(pattern, col_index * blocks_col, blocks_col, 0)
        return jnp.repeat(rows_here, width, axis=1).astype(bf16)[:, None, :]

    def row_mask(pattern, count):
        piece = lax.dynamic_slice(pattern, (row_index, col_index * count), (1, count))
        return jnp.repeat(piece, width, axis=1).astype(f32)

    def owner_block(gathered, count):
        root = row_index // blocks_col
        pick = jnp.clip(row_index - col_index * blocks_col, 0, blocks_col - 1)
        own_all = broadcast(
            lax.dynamic_index_in_dim(gathered, pick, 0, keepdims=False), "col", root
        )
        return lax.dynamic_slice_in_dim(own_all, col_index * count * width, count * width, 1)

    def level_products(gathered, count):
        flat = gathered.reshape(-1, gathered.shape[2])
        summed = lax.psum_scatter(
            lax.dot_general(
                flat, inverse_top, (((0,), (1,)), ((), ())), preferred_element_type=f32
            ),
            "col",
            scatter_dimension=0,
            tiled=True,
        )
        own = owner_block(gathered, count)
        return (summed.T, own)

    masked_first = factor_first * column_mask(pattern_first)
    masked_second = factor_second * column_mask(mask_second)
    gathered_first = spread_factor(masked_first)
    z_first, own_first = level_products(gathered_first, local_first)
    x_first = (-(row_mask(pattern_first, local_first) * z_first)).astype(bf16)
    shape_first = (width, local_first, width)
    partial_first = jnp.einsum(
        "wsa,wsb->sab",
        own_first.reshape(shape_first),
        x_first.reshape(shape_first),
        preferred_element_type=f32,
    )
    summed_first = column_sums(partial_first)
    diag_first = (
        (diag_first_inv.reshape(local_first, width, width) - summed_first)
        .astype(bf16)
        .reshape(-1, width)
    )
    x_all, diag_all = (
        lax.all_gather(x_first, "col", axis=1, tiled=True),
        lax.all_gather(diag_first, "col", axis=0, tiled=True),
    )
    parent_here = lax.dynamic_slice_in_dim(parent, col_index * local_second, local_second, 0)
    select = (parent_here == jnp.arange(total_first, dtype=jnp.int32)[None, :]).astype(bf16)
    x_parent = jnp.einsum(
        "wkb,sk->wsb", x_all.reshape(width, total_first, width), select, preferred_element_type=f32
    ).astype(bf16)
    a_parent = jnp.einsum(
        "kab,sk->sab",
        diag_all.reshape(total_first, width, width),
        select,
        preferred_element_type=f32,
    ).astype(bf16)
    gathered_second = spread_factor(masked_second)
    z_second, own_second = level_products(gathered_second, local_second)
    below = parent_factor.reshape(local_second, width, width)
    z_second = z_second + jnp.einsum(
        "wsa,sab->wsb", x_parent, below, preferred_element_type=f32
    ).reshape(width, -1)
    x_second = (-(row_mask(mask_second, local_second) * z_second)).astype(bf16)
    shape_second = (width, local_second, width)
    own_blocks = own_second.reshape(shape_second)
    cross_part, inner_part = column_sums(
        (
            jnp.einsum("wsa,wsb->sab", x_parent, own_blocks, preferred_element_type=f32),
            jnp.einsum(
                "wsa,wsb->sab",
                own_blocks,
                x_second.reshape(shape_second),
                preferred_element_type=f32,
            ),
        )
    )
    cross = (
        -(cross_part + jnp.einsum("sak,skb->sab", a_parent, below, preferred_element_type=f32))
    ).astype(bf16)
    diag_second = (
        diag_second_inv.reshape(local_second, width, width)
        - inner_part
        - jnp.einsum("sab,sac->sbc", below, cross, preferred_element_type=f32)
    )
    return (x_first, diag_first, x_second, cross.reshape(-1, width), diag_second.reshape(-1, width))


MESH = pl.DeviceIdType.MESH
VMEM_BUDGET = 64 * 1024 * 1024
UP, DOWN, ACROSS, SIB, SIB_FAR = range(5)
INV, ONE, TWO, DIAG = range(4)


def fused_kernel(
    rows,
    cols,
    inv_ref,
    one_ref,
    two_ref,
    below_ref,
    dinv_one_ref,
    dinv_two_ref,
    pat_one,
    pat_two,
    parent,
    x_one_ref,
    diag_one_ref,
    x_two_ref,
    cross_ref,
    diag_two_ref,
    inv_all,
    one_all,
    two_all,
    below_own,
    dinv_one,
    dinv_two,
    diag_all,
    masked,
    x_one_all,
    x_two_all,
    send_sem,
    recv_sem,
    local_sem,
):
    f32, bf16 = jnp.float32, jnp.bfloat16
    width = inv_ref.shape[0]
    slab = one_ref.shape[0]
    y = lax.axis_index("pole")
    z = lax.axis_index("row")
    c = lax.axis_index("col")
    sib = c + 1 - 2 * (c % 2)
    far = (c + 2) % cols
    far_sib = (sib + 2) % cols
    devices = {
        UP: (y, z + 1, c),
        DOWN: (y, z - 1, c),
        ACROSS: (y, z, far),
        SIB: (y, z, sib),
        SIB_FAR: (y, z, sib),
    }

    def span(start, size):
        return pl.ds(pl.multiple_of(start, size), size)

    def columns(lane):
        if lane in (UP, DOWN):
            return slice(None)
        if lane == ACROSS:
            return span((far // 2) * 2 * width, 2 * width)
        return span(sib * width, width)

    def arrived(lane):
        if lane in (UP, DOWN):
            return slice(None)
        if lane == ACROSS:
            return span((c // 2) * 2 * width, 2 * width)
        return span(c * width, width)

    def place(unit, zs, cs, part):
        if unit == INV:
            return inv_all.at[cs, span(zs * width, width), :]
        if unit == ONE:
            return one_all.at[cs, zs]
        if unit == TWO:
            return two_all.at[cs, zs, :, part]
        return diag_all.at[cs]

    def when(conditions, act):
        if conditions:
            both = conditions[0]
            for condition in conditions[1:]:
                both = jnp.logical_and(both, condition)
            pl.when(both)(act)
        else:
            act()

    sent = []

    def send(unit, zs, cs, lane, conditions=()):
        def descriptor():
            part = columns(lane)
            return pltpu.make_async_remote_copy(
                src_ref=place(unit, zs, cs, part),
                dst_ref=place(unit, zs, cs, part),
                send_sem=send_sem.at[unit, zs, lane],
                recv_sem=recv_sem.at[unit, zs, cs],
                device_id=devices[lane],
                device_id_type=MESH,
            )

        when(list(conditions), lambda: descriptor().start())
        sent.append((list(conditions), descriptor))

    def receive(unit, zs, cs, lane, conditions=()):
        def act():
            part = arrived(lane)
            pltpu.make_async_remote_copy(
                src_ref=place(unit, zs, cs, part),
                dst_ref=place(unit, zs, cs, part),
                send_sem=send_sem.at[unit, zs, lane],
                recv_sem=recv_sem.at[unit, zs, cs],
                device_id=devices[SIB],
                device_id_type=MESH,
            ).wait_recv()

        when(list(conditions), act)

    can_up, can_down = z + 1 < rows, z >= 1
    everything = slice(None)
    local = [
        pltpu.make_async_copy(source, target, local_sem.at[slot])
        for slot, (source, target) in enumerate(
            (
                (inv_ref, place(INV, z, c, everything)),
                (one_ref, place(ONE, z, c, everything)),
                (two_ref, place(TWO, z, c, everything)),
                (below_ref, below_own),
                (dinv_one_ref, dinv_one),
                (dinv_two_ref, dinv_two),
            )
        )
    ]
    for copy in local:
        copy.start()

    barrier = pltpu.get_barrier_semaphore()
    for lane, conditions in ((UP, [can_up]), (DOWN, [can_down]), (ACROSS, []), (SIB, [])):
        when(
            conditions,
            lambda lane=lane: pl.semaphore_signal(
                barrier, inc=1, device_id=devices[lane], device_id_type=MESH
            ),
        )
    pl.semaphore_wait(barrier, 2 + can_up.astype(jnp.int32) + can_down.astype(jnp.int32))

    def at_distance(step):
        if step == 0:
            return [(z, [], None, [])]
        return [
            (z - step, [z - step >= 0], UP, [can_up]),
            (z + step, [z + step < rows], DOWN, [can_down]),
        ]

    def send_own(unit):
        local[unit].wait()
        send(unit, z, c, UP, [can_up])
        send(unit, z, c, DOWN, [can_down])
        send(unit, z, c, ACROSS)
        send(unit, z, c, SIB)

    def pass_along(units, step):
        for unit in units:
            for zs, exists, lane, further in at_distance(step):
                receive(unit, zs, c, lane, exists)
                if step < rows - 1:
                    send(unit, zs, c, lane, exists + further)
                send(unit, zs, c, ACROSS, exists)
                send(unit, zs, c, SIB, exists)

    def pass_across(units, step):
        for unit in units:
            for zs, exists, _, _ in at_distance(step):
                receive(unit, zs, far, ACROSS, exists)
                send(unit, zs, far, SIB_FAR, exists)

    def settle(units):
        for unit in units:
            for zs in range(rows):
                receive(unit, zs, sib, SIB)
                receive(unit, zs, far_sib, SIB_FAR)

    first = (INV, ONE)
    for unit in first:
        send_own(unit)
    for step in range(1, rows):
        if step == rows - 1:
            send_own(TWO)
        pass_along(first, step)
    for step in range(1, rows - 1):
        pass_along((TWO,), step)
    for step in range(rows):
        pass_across(first, step)
    settle(first)
    for copy in local[3:]:
        copy.wait()

    chosen = [(parent[c, 0] == k).astype(jnp.int32).astype(f32) for k in range(cols)]

    def mask_one(b):
        return pat_one[b, c].astype(f32)

    def mask_parent(b):
        return sum(chosen[k] * pat_one[b, k].astype(f32) for k in range(cols))

    def mask_two(b):
        return pat_two[b, c].astype(f32) * mask_parent(b)

    def gather_columns(slot, source, mask):
        for b in range(cols):
            block = source[b, :, :, span(c * width, width)].reshape(width, width)
            masked[slot, b] = (block.astype(f32) * mask(b)).astype(bf16)

    def gather_parent():
        for b in range(cols):
            total = None
            for k in range(cols):
                block = one_all[b, :, :, k * width : (k + 1) * width].reshape(width, width)
                term = block.astype(f32) * (chosen[k] * pat_one[b, k].astype(f32))
                total = term if total is None else total + term
            masked[1, b] = total.astype(bf16)

    def dot(a, b, ca=1, cb=0):
        return lax.dot_general(a, b, (((ca,), (cb,)), ((), ())), preferred_element_type=f32)

    def times_inverse(slot, r):
        total = None
        for b in range(cols):
            term = dot(inv_all[b, r * width : (r + 1) * width, :], masked[slot, b])
            total = term if total is None else total + term
        return total

    gather_columns(0, one_all, mask_one)
    gather_parent()
    below = below_own[...]

    inner = jnp.zeros((width, width), f32)
    for r in range(rows):
        x_own = (-(mask_one(r) * times_inverse(0, r))).astype(bf16)
        x_one_all[r] = x_own
        inner += dot(masked[0, r], x_own, 0, 0)
    diag_one = (dinv_one[...] - inner).astype(bf16)
    diag_all[c] = diag_one
    send(DIAG, 0, c, ACROSS)
    send(DIAG, 0, c, SIB)
    pass_along((TWO,), rows - 1)
    for r in range(rows):
        x_two_all[r] = (-(mask_parent(r) * times_inverse(1, r))).astype(bf16)
    for step in range(rows):
        pass_across((TWO,), step)
    receive(DIAG, 0, far, ACROSS)
    send(DIAG, 0, far, SIB_FAR)
    x_one_ref[...] = x_one_all[z]
    diag_one_ref[...] = diag_one
    settle((TWO,))
    gather_columns(2, two_all, mask_two)

    cross_part = jnp.zeros((width, width), f32)
    inner_two = jnp.zeros((width, width), f32)
    for r in range(rows):
        x_par = x_two_all[r]
        cross_part += dot(x_par, masked[2, r], 0, 0)
        z_two = times_inverse(2, r) + dot(x_par, below)
        x_two = (-(mask_two(r) * z_two)).astype(bf16)
        x_two_all[r] = x_two
        inner_two += dot(masked[2, r], x_two, 0, 0)
    x_two_ref[...] = x_two_all[z]
    receive(DIAG, 0, sib, SIB)
    receive(DIAG, 0, far_sib, SIB_FAR)
    diag_parent = sum(chosen[k] * diag_all[k].astype(f32) for k in range(cols)).astype(bf16)
    cross = (-(cross_part + dot(diag_parent, below))).astype(bf16)
    cross_ref[...] = cross
    diag_two_ref[...] = dinv_two[...] - inner_two - dot(below, cross, 0, 0)

    for conditions, descriptor in sent:
        when(conditions, lambda descriptor=descriptor: descriptor().wait_send())


def place_results(*refs):
    count = len(refs) // 2
    for slot in range(count):
        refs[count + slot][...] = refs[slot][...]


def on_device_small(
    rows,
    cols,
    inverse_top,
    factor_first,
    factor_second,
    parent_factor,
    diag_first_inv,
    diag_second_inv,
    pattern_first,
    pattern_second,
    parent,
):
    bf16 = jnp.bfloat16
    width = inverse_top.shape[0]
    slab, wide = factor_first.shape[1:]
    square = (width, width)
    vmem = pl.BlockSpec(memory_space=pltpu.VMEM)
    hbm = pl.BlockSpec(memory_space=pltpu.HBM)
    smem = pl.BlockSpec(memory_space=pltpu.SMEM)
    shape = jax.ShapeDtypeStruct
    results = pl.pallas_call(
        functools.partial(fused_kernel, rows, cols),
        out_shape=(
            shape(square, bf16),
            shape(square, bf16),
            shape(square, bf16),
            shape(square, bf16),
            shape(square, jnp.float32),
        ),
        in_specs=[hbm] * 6 + [smem] * 3,
        out_specs=(vmem,) * 5,
        scratch_shapes=[
            pltpu.VMEM((cols, rows * width, width), bf16),
            pltpu.VMEM((cols, rows, slab, wide), bf16),
            pltpu.VMEM((cols, rows, slab, wide), bf16),
            pltpu.VMEM(square, bf16),
            pltpu.VMEM(square, jnp.float32),
            pltpu.VMEM(square, jnp.float32),
            pltpu.VMEM((cols,) + square, bf16),
            pltpu.VMEM((3, cols) + square, bf16),
            pltpu.VMEM((rows,) + square, bf16),
            pltpu.VMEM((rows,) + square, bf16),
            pltpu.SemaphoreType.DMA((4, rows, 5)),
            pltpu.SemaphoreType.DMA((4, rows, cols)),
            pltpu.SemaphoreType.DMA((6,)),
        ],
        compiler_params=pltpu.CompilerParams(
            collective_id=0, has_side_effects=True, vmem_limit_bytes=VMEM_BUDGET
        ),
    )(
        inverse_top,
        factor_first.reshape(slab, wide),
        factor_second.reshape(slab, wide),
        parent_factor,
        diag_first_inv,
        diag_second_inv,
        pattern_first,
        pattern_second,
        parent,
    )
    return pl.pallas_call(
        place_results,
        out_shape=tuple(shape(result.shape, result.dtype) for result in results),
        in_specs=[vmem] * 5,
        out_specs=(vmem,) * 5,
    )(*results)


def on_device(rows, cols, *args):
    inverse_top, factor_first, factor_second, parent_factor = args[:4]
    width, depth = inverse_top.shape
    one_each = (
        cols == 4
        and depth == width
        and factor_first.shape[0] == 1
        and factor_second.shape == factor_first.shape
        and factor_first.shape[1] % 16 == 0
        and factor_first.shape[2] == cols * width
        and parent_factor.shape[0] == width
        and rows == cols
    )
    gathered = 2 * rows * cols * (inverse_top.size + factor_first.size + factor_second.size)
    if one_each and gathered <= VMEM_BUDGET // 2:
        return on_device_small(rows, cols, *args)
    return on_device_large(*args)


def solution(mesh):
    in_specs = (
        P(("pole", "row"), "col"),
        P(("pole", "col"), "row", None),
        P(("pole", "col"), "row", None),
        P(("pole", "col"), None),
        P(("pole", "col"), None),
        P(("pole", "col"), None),
        P(),
        P(),
        P(),
    )
    out_specs = (
        P(("pole", "row"), "col"),
        P(("pole", "col"), None),
        P(("pole", "row"), "col"),
        P(("pole", "col"), None),
        P(("pole", "col"), None),
    )
    return jax.shard_map(
        functools.partial(on_device, mesh.shape["row"], mesh.shape["col"]), mesh=mesh, in_specs=in_specs, out_specs=out_specs, check_vma=False
    )
```

```python
import functools

import jax
import jax.numpy as jnp
from jax import lax
from jax.experimental import pallas as pl
from jax.experimental.pallas import tpu as pltpu
from jax.sharding import PartitionSpec as P


def broadcast(value, axis, source):
    kept = jnp.where(lax.axis_index(axis) == source, value, 0).astype(value.dtype)
    return lax.psum(kept, axis)


def spread_factor(masked):
    return lax.all_gather(masked, "row", axis=1, tiled=True)


def column_sums(parts):
    return lax.psum(parts, "row")


def on_device_large(
    inverse_top,
    factor_first,
    factor_second,
    parent_factor,
    diag_first_inv,
    diag_second_inv,
    pattern_first,
    pattern_second,
    parent,
):
    f32 = jnp.float32
    bf16 = jnp.bfloat16
    col_index = lax.axis_index("col")
    row_index = lax.axis_index("row")
    width = inverse_top.shape[0]
    blocks_col = factor_first.shape[0]
    local_first = diag_first_inv.shape[0] // width
    local_second = diag_second_inv.shape[0] // width
    total_first = pattern_first.shape[1]
    onehot = (parent == jnp.arange(total_first, dtype=jnp.int32)[None, :]).astype(jnp.int32)
    mask_second = pattern_second * jnp.sum(pattern_first[:, None, :] * onehot[None, :, :], axis=2)

    def column_mask(pattern):
        rows_here = lax.dynamic_slice_in_dim(pattern, col_index * blocks_col, blocks_col, 0)
        return jnp.repeat(rows_here, width, axis=1).astype(bf16)[:, None, :]

    def row_mask(pattern, count):
        piece = lax.dynamic_slice(pattern, (row_index, col_index * count), (1, count))
        return jnp.repeat(piece, width, axis=1).astype(f32)

    def owner_block(gathered, count):
        root = row_index // blocks_col
        pick = jnp.clip(row_index - col_index * blocks_col, 0, blocks_col - 1)
        own_all = broadcast(
            lax.dynamic_index_in_dim(gathered, pick, 0, keepdims=False), "col", root
        )
        return lax.dynamic_slice_in_dim(own_all, col_index * count * width, count * width, 1)

    def level_products(gathered, count):
        flat = gathered.reshape(-1, gathered.shape[2])
        summed = lax.psum_scatter(
            lax.dot_general(
                flat, inverse_top, (((0,), (1,)), ((), ())), preferred_element_type=f32
            ),
            "col",
            scatter_dimension=0,
            tiled=True,
        )
        own = owner_block(gathered, count)
        return (summed.T, own)

    masked_first = factor_first * column_mask(pattern_first)
    masked_second = factor_second * column_mask(mask_second)
    gathered_first = spread_factor(masked_first)
    z_first, own_first = level_products(gathered_first, local_first)
    x_first = (-(row_mask(pattern_first, local_first) * z_first)).astype(bf16)
    shape_first = (width, local_first, width)
    partial_first = jnp.einsum(
        "wsa,wsb->sab",
        own_first.reshape(shape_first),
        x_first.reshape(shape_first),
        preferred_element_type=f32,
    )
    summed_first = column_sums(partial_first)
    diag_first = (
        (diag_first_inv.reshape(local_first, width, width) - summed_first)
        .astype(bf16)
        .reshape(-1, width)
    )
    x_all, diag_all = (
        lax.all_gather(x_first, "col", axis=1, tiled=True),
        lax.all_gather(diag_first, "col", axis=0, tiled=True),
    )
    parent_here = lax.dynamic_slice_in_dim(parent, col_index * local_second, local_second, 0)
    select = (parent_here == jnp.arange(total_first, dtype=jnp.int32)[None, :]).astype(bf16)
    x_parent = jnp.einsum(
        "wkb,sk->wsb", x_all.reshape(width, total_first, width), select, preferred_element_type=f32
    ).astype(bf16)
    a_parent = jnp.einsum(
        "kab,sk->sab",
        diag_all.reshape(total_first, width, width),
        select,
        preferred_element_type=f32,
    ).astype(bf16)
    gathered_second = spread_factor(masked_second)
    z_second, own_second = level_products(gathered_second, local_second)
    below = parent_factor.reshape(local_second, width, width)
    z_second = z_second + jnp.einsum(
        "wsa,sab->wsb", x_parent, below, preferred_element_type=f32
    ).reshape(width, -1)
    x_second = (-(row_mask(mask_second, local_second) * z_second)).astype(bf16)
    shape_second = (width, local_second, width)
    own_blocks = own_second.reshape(shape_second)
    cross_part, inner_part = column_sums(
        (
            jnp.einsum("wsa,wsb->sab", x_parent, own_blocks, preferred_element_type=f32),
            jnp.einsum(
                "wsa,wsb->sab",
                own_blocks,
                x_second.reshape(shape_second),
                preferred_element_type=f32,
            ),
        )
    )
    cross = (
        -(cross_part + jnp.einsum("sak,skb->sab", a_parent, below, preferred_element_type=f32))
    ).astype(bf16)
    diag_second = (
        diag_second_inv.reshape(local_second, width, width)
        - inner_part
        - jnp.einsum("sab,sac->sbc", below, cross, preferred_element_type=f32)
    )
    return (x_first, diag_first, x_second, cross.reshape(-1, width), diag_second.reshape(-1, width))


MESH = pl.DeviceIdType.MESH
VMEM_BUDGET = 64 * 1024 * 1024
UP, DOWN, ACROSS, SIB, SIB_FAR = range(5)
INV, ONE, TWO, DIAG = range(4)


def fused_kernel(
    rows,
    cols,
    inv_ref,
    one_ref,
    two_ref,
    below_ref,
    dinv_one_ref,
    dinv_two_ref,
    pat_one,
    pat_two,
    parent,
    x_one_ref,
    diag_one_ref,
    x_two_ref,
    cross_ref,
    diag_two_ref,
    inv_all,
    one_all,
    two_all,
    below_own,
    dinv_one,
    dinv_two,
    diag_all,
    masked,
    x_one_all,
    x_two_all,
    send_sem,
    recv_sem,
    local_sem,
):
    f32, bf16 = jnp.float32, jnp.bfloat16
    width = inv_ref.shape[0]
    slab = one_ref.shape[0]
    y = lax.axis_index("pole")
    z = lax.axis_index("row")
    c = lax.axis_index("col")
    sib = c + 1 - 2 * (c % 2)
    far = (c + 2) % cols
    far_sib = (sib + 2) % cols
    devices = {
        UP: (y, z + 1, c),
        DOWN: (y, z - 1, c),
        ACROSS: (y, z, far),
        SIB: (y, z, sib),
        SIB_FAR: (y, z, sib),
    }

    def span(start, size):
        return pl.ds(pl.multiple_of(start, size), size)

    def columns(lane):
        if lane in (UP, DOWN):
            return slice(None)
        if lane == ACROSS:
            return span((far // 2) * 2 * width, 2 * width)
        return span(sib * width, width)

    def arrived(lane):
        if lane in (UP, DOWN):
            return slice(None)
        if lane == ACROSS:
            return span((c // 2) * 2 * width, 2 * width)
        return span(c * width, width)

    def place(unit, zs, cs, part):
        if unit == INV:
            return inv_all.at[cs, span(zs * width, width), :]
        if unit == ONE:
            return one_all.at[cs, zs]
        if unit == TWO:
            return two_all.at[cs, zs, :, part]
        return diag_all.at[cs]

    def when(conditions, act):
        if conditions:
            both = conditions[0]
            for condition in conditions[1:]:
                both = jnp.logical_and(both, condition)
            pl.when(both)(act)
        else:
            act()

    sent = []

    def send(unit, zs, cs, lane, conditions=()):
        def descriptor():
            part = columns(lane)
            return pltpu.make_async_remote_copy(
                src_ref=place(unit, zs, cs, part),
                dst_ref=place(unit, zs, cs, part),
                send_sem=send_sem.at[unit, zs, lane],
                recv_sem=recv_sem.at[unit, zs, cs],
                device_id=devices[lane],
                device_id_type=MESH,
            )

        when(list(conditions), lambda: descriptor().start())
        sent.append((list(conditions), descriptor))

    def receive(unit, zs, cs, lane, conditions=()):
        def act():
            part = arrived(lane)
            pltpu.make_async_remote_copy(
                src_ref=place(unit, zs, cs, part),
                dst_ref=place(unit, zs, cs, part),
                send_sem=send_sem.at[unit, zs, lane],
                recv_sem=recv_sem.at[unit, zs, cs],
                device_id=devices[SIB],
                device_id_type=MESH,
            ).wait_recv()

        when(list(conditions), act)

    can_up, can_down = z + 1 < rows, z >= 1
    everything = slice(None)
    local = [
        pltpu.make_async_copy(source, target, local_sem.at[slot])
        for slot, (source, target) in enumerate(
            (
                (inv_ref, place(INV, z, c, everything)),
                (one_ref, place(ONE, z, c, everything)),
                (two_ref, place(TWO, z, c, everything)),
                (below_ref, below_own),
                (dinv_one_ref, dinv_one),
                (dinv_two_ref, dinv_two),
            )
        )
    ]
    for copy in local:
        copy.start()

    barrier = pltpu.get_barrier_semaphore()
    for lane, conditions in ((UP, [can_up]), (DOWN, [can_down]), (ACROSS, []), (SIB, [])):
        when(
            conditions,
            lambda lane=lane: pl.semaphore_signal(
                barrier, inc=1, device_id=devices[lane], device_id_type=MESH
            ),
        )
    pl.semaphore_wait(barrier, 2 + can_up.astype(jnp.int32) + can_down.astype(jnp.int32))

    def at_distance(step):
        if step == 0:
            return [(z, [], None, [])]
        return [
            (z - step, [z - step >= 0], UP, [can_up]),
            (z + step, [z + step < rows], DOWN, [can_down]),
        ]

    def send_own(unit):
        local[unit].wait()
        send(unit, z, c, UP, [can_up])
        send(unit, z, c, DOWN, [can_down])
        send(unit, z, c, ACROSS)
        send(unit, z, c, SIB)

    def pass_along(units, step):
        for unit in units:
            for zs, exists, lane, further in at_distance(step):
                receive(unit, zs, c, lane, exists)
                if step < rows - 1:
                    send(unit, zs, c, lane, exists + further)
                send(unit, zs, c, ACROSS, exists)
                send(unit, zs, c, SIB, exists)

    def pass_across(units, step):
        for unit in units:
            for zs, exists, _, _ in at_distance(step):
                receive(unit, zs, far, ACROSS, exists)
                send(unit, zs, far, SIB_FAR, exists)

    def settle(units):
        for unit in units:
            for zs in range(rows):
                receive(unit, zs, sib, SIB)
                receive(unit, zs, far_sib, SIB_FAR)

    first = (INV, ONE)
    for unit in first:
        send_own(unit)
    for step in range(1, rows):
        if step == rows - 1:
            send_own(TWO)
        pass_along(first, step)
    for step in range(1, rows - 1):
        pass_along((TWO,), step)
    for step in range(rows):
        pass_across(first, step)
    settle(first)
    for copy in local[3:]:
        copy.wait()

    chosen = [(parent[c, 0] == k).astype(jnp.int32).astype(f32) for k in range(cols)]

    def mask_one(b):
        return pat_one[b, c].astype(f32)

    def mask_parent(b):
        return sum(chosen[k] * pat_one[b, k].astype(f32) for k in range(cols))

    def mask_two(b):
        return pat_two[b, c].astype(f32) * mask_parent(b)

    def gather_columns(slot, source, mask):
        for b in range(cols):
            block = source[b, :, :, span(c * width, width)].reshape(width, width)
            masked[slot, b] = (block.astype(f32) * mask(b)).astype(bf16)

    def gather_parent():
        for b in range(cols):
            total = None
            for k in range(cols):
                block = one_all[b, :, :, k * width : (k + 1) * width].reshape(width, width)
                term = block.astype(f32) * (chosen[k] * pat_one[b, k].astype(f32))
                total = term if total is None else total + term
            masked[1, b] = total.astype(bf16)

    def dot(a, b, ca=1, cb=0):
        return lax.dot_general(a, b, (((ca,), (cb,)), ((), ())), preferred_element_type=f32)

    def times_inverse(slot, r):
        total = None
        for b in range(cols):
            term = dot(inv_all[b, r * width : (r + 1) * width, :], masked[slot, b])
            total = term if total is None else total + term
        return total

    gather_columns(0, one_all, mask_one)
    gather_parent()
    below = below_own[...]

    inner = jnp.zeros((width, width), f32)
    for r in range(rows):
        x_own = (-(mask_one(r) * times_inverse(0, r))).astype(bf16)
        x_one_all[r] = x_own
        inner += dot(masked[0, r], x_own, 0, 0)
    diag_one = (dinv_one[...] - inner).astype(bf16)
    diag_all[c] = diag_one
    send(DIAG, 0, c, ACROSS)
    send(DIAG, 0, c, SIB)
    pass_along((TWO,), rows - 1)
    for step in range(rows - 1):
        pass_across((TWO,), step)
    for r in range(rows):
        x_two_all[r] = (-(mask_parent(r) * times_inverse(1, r))).astype(bf16)
    pass_across((TWO,), rows - 1)
    x_one_ref[...] = x_one_all[z]
    diag_one_ref[...] = diag_one
    settle((TWO,))
    receive(DIAG, 0, far, ACROSS)
    send(DIAG, 0, far, SIB_FAR)
    gather_columns(2, two_all, mask_two)

    cross_part = jnp.zeros((width, width), f32)
    inner_two = jnp.zeros((width, width), f32)
    for r in range(rows):
        x_par = x_two_all[r]
        cross_part += dot(x_par, masked[2, r], 0, 0)
        z_two = times_inverse(2, r) + dot(x_par, below)
        x_two = (-(mask_two(r) * z_two)).astype(bf16)
        x_two_all[r] = x_two
        inner_two += dot(masked[2, r], x_two, 0, 0)
    x_two_ref[...] = x_two_all[z]
    receive(DIAG, 0, sib, SIB)
    receive(DIAG, 0, far_sib, SIB_FAR)
    diag_parent = sum(chosen[k] * diag_all[k].astype(f32) for k in range(cols)).astype(bf16)
    cross = (-(cross_part + dot(diag_parent, below))).astype(bf16)
    cross_ref[...] = cross
    diag_two_ref[...] = dinv_two[...] - inner_two - dot(below, cross, 0, 0)

    for conditions, descriptor in sent:
        when(conditions, lambda descriptor=descriptor: descriptor().wait_send())


def place_results(*refs):
    count = len(refs) // 2
    for slot in range(count):
        refs[count + slot][...] = refs[slot][...]


def on_device_small(
    rows,
    cols,
    inverse_top,
    factor_first,
    factor_second,
    parent_factor,
    diag_first_inv,
    diag_second_inv,
    pattern_first,
    pattern_second,
    parent,
):
    bf16 = jnp.bfloat16
    width = inverse_top.shape[0]
    slab, wide = factor_first.shape[1:]
    square = (width, width)
    vmem = pl.BlockSpec(memory_space=pltpu.VMEM)
    hbm = pl.BlockSpec(memory_space=pltpu.HBM)
    smem = pl.BlockSpec(memory_space=pltpu.SMEM)
    shape = jax.ShapeDtypeStruct
    results = pl.pallas_call(
        functools.partial(fused_kernel, rows, cols),
        out_shape=(
            shape(square, bf16),
            shape(square, bf16),
            shape(square, bf16),
            shape(square, bf16),
            shape(square, jnp.float32),
        ),
        in_specs=[hbm] * 6 + [smem] * 3,
        out_specs=(vmem,) * 5,
        scratch_shapes=[
            pltpu.VMEM((cols, rows * width, width), bf16),
            pltpu.VMEM((cols, rows, slab, wide), bf16),
            pltpu.VMEM((cols, rows, slab, wide), bf16),
            pltpu.VMEM(square, bf16),
            pltpu.VMEM(square, jnp.float32),
            pltpu.VMEM(square, jnp.float32),
            pltpu.VMEM((cols,) + square, bf16),
            pltpu.VMEM((3, cols) + square, bf16),
            pltpu.VMEM((rows,) + square, bf16),
            pltpu.VMEM((rows,) + square, bf16),
            pltpu.SemaphoreType.DMA((4, rows, 5)),
            pltpu.SemaphoreType.DMA((4, rows, cols)),
            pltpu.SemaphoreType.DMA((6,)),
        ],
        compiler_params=pltpu.CompilerParams(
            collective_id=0, has_side_effects=True, vmem_limit_bytes=VMEM_BUDGET
        ),
    )(
        inverse_top,
        factor_first.reshape(slab, wide),
        factor_second.reshape(slab, wide),
        parent_factor,
        diag_first_inv,
        diag_second_inv,
        pattern_first,
        pattern_second,
        parent,
    )
    return pl.pallas_call(
        place_results,
        out_shape=tuple(shape(result.shape, result.dtype) for result in results),
        in_specs=[vmem] * 5,
        out_specs=(vmem,) * 5,
    )(*results)


def on_device(rows, cols, *args):
    inverse_top, factor_first, factor_second, parent_factor = args[:4]
    width, depth = inverse_top.shape
    one_each = (
        cols == 4
        and depth == width
        and factor_first.shape[0] == 1
        and factor_second.shape == factor_first.shape
        and factor_first.shape[1] % 16 == 0
        and factor_first.shape[2] == cols * width
        and parent_factor.shape[0] == width
        and rows == cols
    )
    gathered = 2 * rows * cols * (inverse_top.size + factor_first.size + factor_second.size)
    if one_each and gathered <= VMEM_BUDGET // 2:
        return on_device_small(rows, cols, *args)
    return on_device_large(*args)


def solution(mesh):
    in_specs = (
        P(("pole", "row"), "col"),
        P(("pole", "col"), "row", None),
        P(("pole", "col"), "row", None),
        P(("pole", "col"), None),
        P(("pole", "col"), None),
        P(("pole", "col"), None),
        P(),
        P(),
        P(),
    )
    out_specs = (
        P(("pole", "row"), "col"),
        P(("pole", "col"), None),
        P(("pole", "row"), "col"),
        P(("pole", "col"), None),
        P(("pole", "col"), None),
    )
    return jax.shard_map(
        functools.partial(on_device, mesh.shape["row"], mesh.shape["col"]), mesh=mesh, in_specs=in_specs, out_specs=out_specs, check_vma=False
    )
```
